256 devices in a mesh: src: 16 (over y_hi, x, core), dst: 16 (over y_lo, z).
Axes of the slice: x: 4, y: 4 (y_hi: 2, y_lo: 2; y = y_hi * 2 + y_lo), z: 8, core: 2. Of those that a mesh axis runs over, the one named last changes fastest.
Arguments:
- source_table: float32 [16384, 400], P(('src', 'dst')), may hold values from -1.5 to 1.5
- source_state: float32 [16384], P(('src', 'dst')), may hold values from 0.02 to 0.2
- target_table: float32 [16384, 400], P(('dst', 'src')), may hold values from -1.5 to 1.5
- target_state: float32 [16384], P(('dst', 'src')), may hold values from 0.02 to 0.2
- relations: bfloat16 [4, 400, 400], replicated, may hold values from -0.3125 to 0.3125
- edge_source: int32 [16, 16, 6144], P('src', 'dst'), may hold values from 0 to 1023
- edge_target: int32 [16, 16, 6144], P('src', 'dst'), may hold values from 0 to 1023
- batch_relation: int32 [16, 16, 12], P('src', 'dst'), may hold values from 0 to 3
- edge_counts: int32 [16, 16], P('src', 'dst'), may hold values from 768 to 6144, as said below
- negatives: int32 [16, 16, 12, 512], P('src', 'dst'), may hold values from 0 to 1023
Outputs:
- new_source_table: float32 [16384, 400], P(('src', 'dst'))
- new_source_state: float32 [16384], P(('src', 'dst'))
- new_target_table: float32 [16384, 400], P(('dst', 'src'))
- new_target_state: float32 [16384], P(('dst', 'src'))
The draws below stay inside these ranges and needn't reach their ends.
Inputs may be any that keep to these rules, and one draw needn't show every extreme that they name: Only slots 0 to edge_counts[i, j] - 1 of a bucket are edges; some bucket holds 6144 in every draw.
All inputs are finite; a program needn't handle non-finite values.
Results may differ from the reference program's by a relative error of at most 0.0065.
Values may be sent and summed in bfloat16 or wider, within the bound.
No kernel may reach another device: no remote copies, remote signals or barrier semaphores. Data moves between devices by JAX's collectives and lax.ppermute only.
A program may use at most 64 MiB of HBM per device.

```python
import math
import jax
import jax.numpy as jnp
from jax import lax

D = 400
NREL = 4
BATCH = 512
NEG = 512
BATCHES = 12
SRC_PART = 1024
DST_PART = 1024
SRC_ENT = 16384
DST_ENT = 16384
CAP = 6144
N_SRC = 16
N_DST = 16


def draw_edge_counts(key, part):
    key = jax.random.fold_in(key, 11)
    first, second, third, fourth = jax.random.split(key, 4)
    light_load = jax.random.randint(first, (N_SRC, N_DST), CAP // 8, CAP // 2 + 1)
    heavy_load = jax.random.randint(second, (N_SRC, N_DST), 3 * CAP // 4, CAP + 1)
    picked = jax.random.randint(third, (N_SRC, N_DST), 0, 8) == 0
    loads = jnp.where(picked, heavy_load, light_load).reshape(-1)
    busiest = jax.random.randint(fourth, (), 0, N_SRC * N_DST)
    loads = loads.at[busiest].set(CAP)
    return loads.reshape(N_SRC, N_DST).astype(jnp.int32)


def place_ends(array, rng, least, largest):
    dims = array.shape
    spot = [jax.random.randint(jax.random.fold_in(rng, axis), (), 0, dims[axis]) for axis in range(len(dims))]
    array = array.at[tuple(spot)].set(least)
    longest = dims.index(max(dims))
    spot[longest] = (spot[longest] + 1) % dims[longest]
    return array.at[tuple(spot)].set(largest)


def steps_of(stream_key, shape, shards, least, high):
    def one(dim, blocks):
        draws = jax.random.uniform(jax.random.fold_in(jax.random.fold_in(stream_key, 6), dim), (blocks,), jnp.float32, least / len(shards), high / len(shards))
        return jnp.repeat(jnp.exp(draws), shape[dim] // blocks).reshape((-1,) + (1,) * (len(shape) - dim - 1))

    factor_of = one(*shards[0])
    for cut in shards[1:]:
        factor_of = factor_of * one(*cut)
    return factor_of


def noise(key, shape, deviation, bound, pieces=(), kind=jnp.bfloat16):
    entries = deviation * jax.random.normal(key, shape, jnp.float32)
    if pieces:
        entries = entries * steps_of(key, shape, pieces, -0.22, 0.18)
    return jnp.clip(entries, -bound, bound).astype(kind)


def setup_inputs(seed: int = 0) -> dict:
    arg_keys = jax.random.split(jax.random.key(seed), 11)
    return {
        "source_table": noise(arg_keys[0], (SRC_ENT, D), 0.25, 1.5, ((0, 256),), jnp.float32),
        "source_state": jnp.clip(jnp.exp(math.log(0.2) - 2.3025851 * jax.random.uniform(arg_keys[1], (SRC_ENT,), jnp.float32) ** steps_of(arg_keys[1], (SRC_ENT,), ((0, 256),), -0.2, 0.2)), 0.02, 0.2),
        "target_table": noise(arg_keys[2], (DST_ENT, D), 0.25, 1.5, ((0, 256),), jnp.float32),
        "target_state": jnp.clip(jnp.exp(math.log(0.2) - 2.3025851 * jax.random.uniform(arg_keys[3], (DST_ENT,), jnp.float32) ** steps_of(arg_keys[3], (DST_ENT,), ((0, 256),), -0.2, 0.2)), 0.02, 0.2),
        "relations": noise(arg_keys[4], (NREL, D, D), D ** -0.5, 0.3125),
        "edge_source": place_ends(jax.random.randint(arg_keys[5], (N_SRC, N_DST, CAP), 0, SRC_PART), jax.random.fold_in(arg_keys[5], 1), 0, SRC_PART - 1).astype(jnp.int32),
        "edge_target": place_ends(jax.random.randint(arg_keys[6], (N_SRC, N_DST, CAP), 0, DST_PART), jax.random.fold_in(arg_keys[6], 1), 0, DST_PART - 1).astype(jnp.int32),
        "batch_relation": place_ends(jax.random.randint(arg_keys[7], (N_SRC, N_DST, BATCHES), 0, NREL), jax.random.fold_in(arg_keys[7], 1), 0, NREL - 1).astype(jnp.int32),
        "edge_counts": draw_edge_counts(jax.random.fold_in(arg_keys[10], 71), 0),
        "negatives": place_ends(jax.random.randint(arg_keys[9], (N_SRC, N_DST, BATCHES, NEG), 0, DST_PART), jax.random.fold_in(arg_keys[9], 1), 0, DST_PART - 1).astype(jnp.int32),
    }


learn_rate = 0.5
epsilon = 1e-08

def make_queries(sources_all, source_ids, relation):
    rows_taken = sources_all[source_ids]
    return jnp.dot(rows_taken, relation, preferred_element_type=jnp.float32).astype(jnp.bfloat16)

def source_back(query_grad, relation):
    return lax.dot_general(query_grad.astype(jnp.bfloat16), relation, (((1,), (1,)), ((), ())), preferred_element_type=jnp.float32)

def score_batch(queries, target_ids, negative_ids, weights, targets_all, target_acc):
    targets = targets_all[target_ids]
    negative_rows = targets_all[negative_ids]
    positive = lax.optimization_barrier(jnp.sum(queries.astype(jnp.float32) * targets.astype(jnp.float32), axis=1))
    negative = lax.dot_general(queries, negative_rows, (((1,), (1,)), ((), ())), preferred_element_type=jnp.float32)
    pos_coef = -weights * jax.nn.sigmoid(-positive)
    neg_coef = (weights[:, None] * jax.nn.sigmoid(negative) / NEG).astype(jnp.bfloat16)
    query_grad = pos_coef[:, None] * targets.astype(jnp.float32) + jnp.dot(neg_coef, negative_rows, preferred_element_type=jnp.float32)
    target_term = pos_coef[:, None] * queries.astype(jnp.float32)
    negative_term = lax.dot_general(neg_coef, queries, (((0,), (0,)), ((), ())), preferred_element_type=jnp.float32)
    target_acc = target_acc.at[target_ids].add(target_term).at[negative_ids].add(negative_term)
    return (query_grad, target_acc)

def adagrad(table, state, grad):
    new_state = state + lax.optimization_barrier(jnp.mean(grad * grad, axis=1))
    return (table - learn_rate * grad / (jnp.sqrt(new_state)[:, None] + epsilon), new_state)

def reference(source_table, source_state, target_table, target_state, relations, edge_source, edge_target, batch_relation, edge_counts, negatives):
    source_parts = source_table.astype(jnp.bfloat16).reshape(N_SRC, SRC_PART, D)
    target_parts = target_table.astype(jnp.bfloat16).reshape(N_DST, DST_PART, D)
    offsets = jnp.arange(BATCH, dtype=jnp.int32)

    def bucket(index, accums):
        source_grad, target_grad = accums
        row_index = (index // N_DST).astype(jnp.int32)
        column_index = (index % N_DST).astype(jnp.int32)
        sources_all = source_parts[row_index]
        targets_all = target_parts[column_index]
        valid_edges = edge_counts[row_index, column_index]
        source_lists = edge_source[row_index, column_index].reshape(BATCHES, BATCH)
        target_lists = edge_target[row_index, column_index].reshape(BATCHES, BATCH)
        relation_list = batch_relation[row_index, column_index]
        negative_lists = negatives[row_index, column_index]

        def one_batch(position, inner):
            source_acc, target_acc = inner
            relation = relations[relation_list[position]]
            queries = make_queries(sources_all, source_lists[position], relation)
            weights = (position * BATCH + offsets < valid_edges).astype(jnp.float32)
            query_grad, target_acc = score_batch(queries, target_lists[position], negative_lists[position], weights, targets_all, target_acc)
            source_acc = source_acc.at[source_lists[position]].add(source_back(query_grad, relation))
            return (source_acc, target_acc)
        batch_total = (valid_edges + BATCH - 1) // BATCH
        source_acc, target_acc = lax.fori_loop(0, batch_total, one_batch, (source_grad[row_index], target_grad[column_index]))
        return (source_grad.at[row_index].set(source_acc), target_grad.at[column_index].set(target_acc))
    start = (jnp.zeros((N_SRC, SRC_PART, D), jnp.float32), jnp.zeros((N_DST, DST_PART, D), jnp.float32))
    source_grad, target_grad = lax.fori_loop(0, N_SRC * N_DST, bucket, start)
    new_source_table, new_source_state = adagrad(source_table, source_state, source_grad.reshape(SRC_ENT, D))
    new_target_table, new_target_state = adagrad(target_table, target_state, target_grad.reshape(DST_ENT, D))
    return (new_source_table, new_source_state, new_target_table, new_target_state)
```

```python
import functools

import jax
import jax.numpy as jnp
from jax import lax
from jax.experimental import pallas as pl
from jax.experimental.pallas import tpu as pltpu
from jax.sharding import PartitionSpec as P

BATCH = 512
NEG = 512
BATCHES = 12
NREL = 4
PART = 1024
DIM = 400
GROUP = 16
TILE = 256

learn_rate = 0.5
epsilon = 1e-08

NT = (((1,), (1,)), ((), ()))
TN = (((0,), (0,)), ((), ()))
VMEM_LIMIT = 56 * 1024 * 1024


def dot(a, b, dims=(((1,), (0,)), ((), ()))):
    return lax.dot_general(a, b, dims, preferred_element_type=jnp.float32)


def one_hot_columns(ids, rows, first, value):
    row = lax.broadcasted_iota(jnp.int32, (rows, ids.shape[1]), 0) + first
    return jnp.where(row == ids, jnp.float32(value), jnp.float32(0.0)).astype(jnp.bfloat16)


def histogram(ids, value):
    high = one_hot_columns(jnp.right_shift(ids, 7), 8, 0, 1.0)
    low = one_hot_columns(jnp.bitwise_and(ids, 127), 128, 0, value)
    table = dot(high, low, NT)
    return jnp.concatenate([table[k : k + 1] for k in range(8)], axis=1)


def count_kernel(rel_ref, cnt_ref, es_ref, et_ref, neg_ref, n_ref, m_ref, ohs, acc, srch, negh):
    step = pl.program_id(0)
    valid = cnt_ref[0]

    @pl.when(step == 0)
    def _():
        srch[...] = jnp.zeros_like(srch)
        negh[...] = jnp.zeros_like(negh)
        slot = lax.broadcasted_iota(jnp.int32, (1, BATCH), 1)
        batch_row = lax.broadcasted_iota(jnp.int32, (16, PART), 0)

        @pl.loop(0, BATCHES)
        def _(b):
            @pl.when(b * BATCH < valid)
            def _():
                at = pl.ds(pl.multiple_of(b * BATCH, BATCH), BATCH)
                ids = jnp.where(slot + b * BATCH < valid, es_ref[:, at], -1)
                ohs[b] = one_hot_columns(ids, PART, 0, 1.0)
                srch[...] = jnp.where(batch_row == b, histogram(ids, 1.0), srch[...])
                negh[...] = jnp.where(batch_row == b, histogram(neg_ref[:, at], 1.0 / 1024.0), negh[...])

    acc[...] = jnp.zeros_like(acc)

    @pl.loop(0, BATCHES)
    def _(b):
        @pl.when(b * BATCH < valid)
        def _():
            at = pl.ds(pl.multiple_of(b * BATCH, BATCH), BATCH)
            oht = one_hot_columns(et_ref[:, at], TILE, step * TILE, 0.5)
            r = rel_ref[b]
            acc[r] += dot(oht, ohs[b], NT)

    n_ref[...] = acc[...].astype(jnp.bfloat16)
    lanes = pl.ds(pl.multiple_of(step * TILE, TILE), TILE)
    negs = negh[:, lanes].astype(jnp.bfloat16)
    row = lax.broadcasted_iota(jnp.int32, (16, 1), 0)
    rel = jnp.full((16, 1), -1, jnp.int32)
    for b in range(BATCHES):
        rel = jnp.where(row == b, rel_ref[b], rel)
    for r in range(NREL):
        kept = jnp.where(rel == r, srch[...], 0.0).astype(jnp.bfloat16)
        m_ref[r] = dot(negs, kept, TN).astype(jnp.bfloat16)


def counts(rel, cnt, es, et, neg):
    smem = pl.BlockSpec(memory_space=pltpu.SMEM)
    whole = pl.BlockSpec((1, BATCHES * BATCH), lambda t: (0, 0))
    tiles = pl.BlockSpec((NREL, TILE, PART), lambda t: (0, t, 0))
    out = jax.ShapeDtypeStruct((NREL, PART, PART), jnp.bfloat16)
    return pl.pallas_call(
        count_kernel,
        grid=(PART // TILE,),
        in_specs=[smem, smem, whole, whole, whole],
        out_specs=[tiles, tiles],
        out_shape=[out, out],
        scratch_shapes=[
            pltpu.VMEM((BATCHES, PART, BATCH), jnp.bfloat16),
            pltpu.VMEM((NREL, TILE, PART), jnp.float32),
            pltpu.VMEM((16, PART), jnp.float32),
            pltpu.VMEM((16, PART), jnp.float32),
        ],
        compiler_params=pltpu.CompilerParams(vmem_limit_bytes=VMEM_LIMIT),
        cost_estimate=pl.CostEstimate(flops=2 * PART * PART * BATCHES * BATCH, bytes_accessed=16 << 20, transcendentals=0),
        name="pair_counts",
    )(rel, cnt, es, et, neg)


def score_kernel(s_ref, t_ref, rel_ref, n_ref, m_ref, gs_ref, gt_ref, q, tt, dqt, sacc, tacc):
    r, k = pl.program_id(0), pl.program_id(1)
    relation = rel_ref[0]

    @pl.when((r == 0) & (k == 0))
    def _():
        tt[...] = t_ref[...].astype(jnp.float32).T.astype(jnp.bfloat16)
        sacc[...] = jnp.zeros_like(sacc)
        tacc[...] = jnp.zeros_like(tacc)

    @pl.when(k == 0)
    def _():
        q[...] = dot(s_ref[...], relation).astype(jnp.bfloat16)
        dqt[...] = jnp.zeros_like(dqt)

    rows = pl.ds(pl.multiple_of(k * TILE, TILE), TILE)
    half = t_ref[rows] * jnp.bfloat16(0.5)
    th = jnp.tanh(dot(half, q[...], NT))
    coef = n_ref[0].astype(jnp.float32) * (th - 1.0) + m_ref[0].astype(jnp.float32) * (th + 1.0)
    coef = coef.astype(jnp.bfloat16)
    tacc[rows] += dot(coef, q[...])
    dqt[...] += dot(tt[:, rows], coef)

    @pl.when(k == pl.num_programs(1) - 1)
    def _():
        sacc[...] += dot(relation, dqt[...].astype(jnp.bfloat16))

    @pl.when((r == pl.num_programs(0) - 1) & (k == pl.num_programs(1) - 1))
    def _():
        gs_ref[...] = sacc[...].T.astype(jnp.bfloat16)
        gt_ref[...] = tacc[...].astype(jnp.bfloat16)


def gradients(sources, targets, relations, n, m):
    whole = pl.BlockSpec((PART, DIM), lambda r, k: (0, 0))
    tiles = pl.BlockSpec((1, TILE, PART), lambda r, k: (r, k, 0))
    out = jax.ShapeDtypeStruct((PART, DIM), jnp.bfloat16)
    return pl.pallas_call(
        score_kernel,
        grid=(NREL, PART // TILE),
        in_specs=[whole, whole, pl.BlockSpec((1, DIM, DIM), lambda r, k: (r, 0, 0)), tiles, tiles],
        out_specs=[whole, whole],
        out_shape=[out, out],
        scratch_shapes=[
            pltpu.VMEM((PART, DIM), jnp.bfloat16),
            pltpu.VMEM((DIM, PART), jnp.bfloat16),
            pltpu.VMEM((DIM, PART), jnp.float32),
            pltpu.VMEM((DIM, PART), jnp.float32),
            pltpu.VMEM((PART, DIM), jnp.float32),
        ],
        compiler_params=pltpu.CompilerParams(vmem_limit_bytes=VMEM_LIMIT),
        cost_estimate=pl.CostEstimate(flops=16 << 30, bytes_accessed=20 << 20, transcendentals=4 << 20),
        name="gradients",
    )(sources, targets, relations, n, m)


def update_kernel(part_ref, table_ref, state_ref, new_table_ref, new_state_ref):
    grad = part_ref[0].astype(jnp.float32)
    for k in range(1, GROUP):
        grad = grad + part_ref[k].astype(jnp.float32)
    rows = grad.shape[0]
    mean = jnp.sum(grad * grad, axis=1, keepdims=True) / DIM
    mean_row = jnp.broadcast_to(mean, (rows, 128)).T[:1]
    new_state_row = state_ref[...] + mean_row
    new_state_ref[...] = new_state_row
    new_state = jnp.broadcast_to(new_state_row, (128, rows)).T[:, :1]
    new_table_ref[...] = table_ref[...] - learn_rate * grad / (jnp.sqrt(new_state) + epsilon)


def update(parts, table, state):
    rows = table.shape[0]
    new_table, new_state = pl.pallas_call(
        update_kernel,
        out_shape=[jax.ShapeDtypeStruct(table.shape, jnp.float32), jax.ShapeDtypeStruct((1, rows), jnp.float32)],
        cost_estimate=pl.CostEstimate(flops=1 << 20, bytes_accessed=2 << 20, transcendentals=0),
        name="row_adagrad",
    )(parts, table, state.reshape(1, rows))
    return new_table, new_state.reshape(rows)


def spread(table, axis):
    rows = table.astype(jnp.bfloat16)
    blocks = jnp.broadcast_to(rows[None], (GROUP,) + rows.shape)
    return lax.all_to_all(blocks, axis, 0, 0).reshape(GROUP * rows.shape[0], rows.shape[1])


def per_device(
    source_table,
    source_state,
    target_table,
    target_state,
    relations,
    edge_source,
    edge_target,
    batch_relation,
    edge_counts,
    negatives,
):
    sources_all = spread(source_table, "dst")
    targets_all = spread(target_table, "src")
    slots = (1, BATCHES * BATCH)
    n, m = counts(
        batch_relation.reshape(BATCHES),
        edge_counts.reshape(1),
        edge_source.reshape(slots),
        edge_target.reshape(slots),
        negatives.reshape(slots),
    )
    source_grad, target_grad = gradients(sources_all, targets_all, relations, n, m)
    rows = source_table.shape[0]
    source_parts = lax.all_to_all(source_grad.reshape(GROUP, rows, DIM), "dst", 0, 0)
    target_parts = lax.all_to_all(target_grad.reshape(GROUP, rows, DIM), "src", 0, 0)
    new_source_table, new_source_state = update(source_parts, source_table, source_state)
    new_target_table, new_target_state = update(target_parts, target_table, target_state)
    return (new_source_table, new_source_state, new_target_table, new_target_state)


def solution(mesh):
    return jax.shard_map(
        per_device,
        mesh=mesh,
        in_specs=(
            P(("src", "dst"), None),
            P(("src", "dst")),
            P(("dst", "src"), None),
            P(("dst", "src")),
            P(),
            P("src", "dst", None),
            P("src", "dst", None),
            P("src", "dst", None),
            P("src", "dst"),
            P("src", "dst", None, None),
        ),
        out_specs=(
            P(("src", "dst"), None),
            P(("src", "dst")),
            P(("dst", "src"), None),
            P(("dst", "src")),
        ),
        check_vma=False,
    )
```

```python
import jax
import jax.numpy as jnp
from jax import lax
from jax.experimental import pallas as pl
from jax.experimental.pallas import tpu as pltpu
from jax.sharding import PartitionSpec as P

BATCH = 512
NEG = 512
BATCHES = 12
NREL = 4
PART = 1024
DIM = 400
GROUP = 16
LINES = 208
TILE = 256

learn_rate = 0.5
epsilon = 1e-08

NT = (((1,), (1,)), ((), ()))
TN = (((0,), (0,)), ((), ()))
VMEM_LIMIT = 56 * 1024 * 1024


def dot(a, b, dims=(((1,), (0,)), ((), ()))):
    return lax.dot_general(a, b, dims, preferred_element_type=jnp.float32)


def one_hot_columns(ids, rows, first, value):
    row = lax.broadcasted_iota(jnp.int32, (rows, ids.shape[1]), 0) + first
    return jnp.where(row == ids, jnp.float32(value), jnp.float32(0.0)).astype(jnp.bfloat16)


def histogram(ids, value):
    high = one_hot_columns(jnp.right_shift(ids, 7), 8, 0, 1.0)
    low = one_hot_columns(jnp.bitwise_and(ids, 127), 128, 0, value)
    table = dot(high, low, NT)
    return jnp.concatenate([table[k : k + 1] for k in range(8)], axis=1)


def count_kernel(rel_ref, cnt_ref, es_ref, et_ref, neg_ref, n_ref, m_ref, ohs, acc, srch, negh):
    step = pl.program_id(0)
    valid = cnt_ref[0]

    @pl.when(step == 0)
    def _():
        srch[...] = jnp.zeros_like(srch)
        negh[...] = jnp.zeros_like(negh)
        slot = lax.broadcasted_iota(jnp.int32, (1, BATCH), 1)
        batch_row = lax.broadcasted_iota(jnp.int32, (16, PART), 0)

        @pl.loop(0, BATCHES)
        def _(b):
            @pl.when(b * BATCH < valid)
            def _():
                at = pl.ds(pl.multiple_of(b * BATCH, BATCH), BATCH)
                ids = jnp.where(slot + b * BATCH < valid, es_ref[:, at], -1)
                ohs[b] = one_hot_columns(ids, PART, 0, 1.0)
                srch[...] = jnp.where(batch_row == b, histogram(ids, 1.0), srch[...])
                negh[...] = jnp.where(batch_row == b, histogram(neg_ref[:, at], 1.0 / 1024.0), negh[...])

    acc[...] = jnp.zeros_like(acc)

    @pl.loop(0, BATCHES)
    def _(b):
        @pl.when(b * BATCH < valid)
        def _():
            at = pl.ds(pl.multiple_of(b * BATCH, BATCH), BATCH)
            oht = one_hot_columns(et_ref[:, at], TILE, step * TILE, 0.5)
            r = rel_ref[b]
            acc[r] += dot(oht, ohs[b], NT)

    n_ref[...] = acc[...].astype(jnp.bfloat16)
    lanes = pl.ds(pl.multiple_of(step * TILE, TILE), TILE)
    negs = negh[:, lanes].astype(jnp.bfloat16)
    row = lax.broadcasted_iota(jnp.int32, (16, 1), 0)
    rel = jnp.full((16, 1), -1, jnp.int32)
    for b in range(BATCHES):
        rel = jnp.where(row == b, rel_ref[b], rel)
    for r in range(NREL):
        kept = jnp.where(rel == r, srch[...], 0.0).astype(jnp.bfloat16)
        m_ref[r] = dot(negs, kept, TN).astype(jnp.bfloat16)


def counts(rel, cnt, es, et, neg):
    smem = pl.BlockSpec(memory_space=pltpu.SMEM)
    whole = pl.BlockSpec((1, BATCHES * BATCH), lambda t: (0, 0))
    tiles = pl.BlockSpec((NREL, TILE, PART), lambda t: (0, t, 0))
    out = jax.ShapeDtypeStruct((NREL, PART, PART), jnp.bfloat16)
    return pl.pallas_call(
        count_kernel,
        grid=(PART // TILE,),
        in_specs=[smem, smem, whole, whole, whole],
        out_specs=[tiles, tiles],
        out_shape=[out, out],
        scratch_shapes=[
            pltpu.VMEM((BATCHES, PART, BATCH), jnp.bfloat16),
            pltpu.VMEM((NREL, TILE, PART), jnp.float32),
            pltpu.VMEM((16, PART), jnp.float32),
            pltpu.VMEM((16, PART), jnp.float32),
        ],
        compiler_params=pltpu.CompilerParams(vmem_limit_bytes=VMEM_LIMIT),
        cost_estimate=pl.CostEstimate(flops=2 * PART * PART * BATCHES * BATCH, bytes_accessed=16 << 20, transcendentals=0),
        name="pair_counts",
    )(rel, cnt, es, et, neg)


def pack(block):
    parts = [block[:, 128 * c : 128 * c + 128] for c in range(3)]
    tail = [block[16 * g : 16 * g + 16, 384:DIM] for g in range(4)]
    parts.append(jnp.concatenate(tail + [jnp.zeros((16, 64), block.dtype)], axis=1))
    return jnp.concatenate(parts, axis=0)


def unpack(lines):
    parts = [lines[64 * c : 64 * c + 64] for c in range(3)]
    tail = [lines[192:208, 16 * g : 16 * g + 16] for g in range(4)]
    parts.append(jnp.concatenate(tail, axis=0))
    return jnp.concatenate(parts, axis=1)


def pack_kernel(source_ref, target_ref, spread_ref, packed_ref):
    lines = pack(source_ref[...]).astype(jnp.bfloat16)
    for d in range(GROUP):
        spread_ref[d] = lines
    packed_ref[...] = pack(target_ref[...]).astype(jnp.bfloat16)


def pack_tables(source_table, target_table):
    return pl.pallas_call(
        pack_kernel,
        out_shape=[
            jax.ShapeDtypeStruct((GROUP, LINES, 128), jnp.bfloat16),
            jax.ShapeDtypeStruct((LINES, 128), jnp.bfloat16),
        ],
        name="pack_tables",
    )(source_table, target_table)


def place(member, near, other):
    high, x, core = member // 8, (member // 2) % 4, member % 2
    return jnp.bitwise_xor(high, near % 2) * 8 + ((x + 4 - near // 2) % 4) * 2 + jnp.bitwise_xor(core, other)


def score_kernel(member_ref, s_ref, t_own_ref, t_other_ref, rel_ref, n_ref, m_ref, gs_ref, a_ref, q_ref, s, t, tt, dqt, sacc):
    r, k = pl.program_id(0), pl.program_id(1)
    relation = rel_ref[0]

    @pl.when((r == 0) & (k == 0))
    def _():
        for d in range(GROUP):
            s[64 * d : 64 * d + 64] = unpack(s_ref[d])
        for other, ref in enumerate((t_own_ref, t_other_ref)):
            for near in range(8):
                first = pl.multiple_of(place(member_ref[0], near, other) * 64, 64)
                t[pl.ds(first, 64)] = unpack(ref[near])
        tt[...] = t[...].astype(jnp.float32).T.astype(jnp.bfloat16)
        sacc[...] = jnp.zeros_like(sacc)

    @pl.when(k == 0)
    def _():
        q_ref[0] = dot(s[...], relation).astype(jnp.bfloat16)
        dqt[...] = jnp.zeros_like(dqt)

    rows = pl.ds(pl.multiple_of(k * TILE, TILE), TILE)
    half = t[rows] * jnp.bfloat16(0.5)
    th = jnp.tanh(dot(half, q_ref[0], NT))
    coef = n_ref[0].astype(jnp.float32) * (th - 1.0) + m_ref[0].astype(jnp.float32) * (th + 1.0)
    coef = coef.astype(jnp.bfloat16)
    a_ref[0] = coef
    dqt[...] += dot(tt[:, rows], coef)

    @pl.when(k == pl.num_programs(1) - 1)
    def _():
        sacc[...] += dot(relation, dqt[...].astype(jnp.bfloat16))

    @pl.when((r == pl.num_programs(0) - 1) & (k == pl.num_programs(1) - 1))
    def _():
        for d in range(0, GROUP, 2):
            pair = sacc[:, 64 * d : 64 * d + 128].T.astype(jnp.bfloat16)
            gs_ref[d] = pack(pair[:64])
            gs_ref[d + 1] = pack(pair[64:])


def source_gradients(member, sources, targets_own, targets_other, relations, n, m):
    tiles = pl.BlockSpec((1, TILE, PART), lambda r, k: (r, k, 0))
    blocks = lambda count: pl.BlockSpec((count, LINES, 128), lambda r, k: (0, 0, 0))
    return pl.pallas_call(
        score_kernel,
        grid=(NREL, PART // TILE),
        in_specs=[
            pl.BlockSpec(memory_space=pltpu.SMEM),
            blocks(GROUP),
            blocks(8),
            blocks(8),
            pl.BlockSpec((1, DIM, DIM), lambda r, k: (r, 0, 0)),
            tiles,
            tiles,
        ],
        out_specs=[blocks(GROUP), tiles, pl.BlockSpec((1, PART, DIM), lambda r, k: (r, 0, 0))],
        out_shape=[
            jax.ShapeDtypeStruct((GROUP, LINES, 128), jnp.bfloat16),
            jax.ShapeDtypeStruct((NREL, PART, PART), jnp.bfloat16),
            jax.ShapeDtypeStruct((NREL, PART, DIM), jnp.bfloat16),
        ],
        scratch_shapes=[
            pltpu.VMEM((PART, DIM), jnp.bfloat16),
            pltpu.VMEM((PART, DIM), jnp.bfloat16),
            pltpu.VMEM((DIM, PART), jnp.bfloat16),
            pltpu.VMEM((DIM, PART), jnp.float32),
            pltpu.VMEM((DIM, PART), jnp.float32),
        ],
        compiler_params=pltpu.CompilerParams(vmem_limit_bytes=VMEM_LIMIT),
        cost_estimate=pl.CostEstimate(flops=12 << 30, bytes_accessed=32 << 20, transcendentals=4 << 20),
        name="source_gradients",
    )(member, sources, targets_own, targets_other, relations, n, m)


def target_kernel(member_ref, a_ref, q_ref, own_ref, other_ref):
    step = pl.program_id(0)
    member = member_ref[0]
    high, x, core = member // 8, (member // 2) % 4, member % 2
    grad = dot(a_ref[0], q_ref[0])
    for r in range(1, NREL):
        grad = grad + dot(a_ref[r], q_ref[r])
    grad = grad.astype(jnp.bfloat16)
    for u in range(4):
        at = step * 4 + u
        near = (((at // 2) % 4 + 4 - x) % 4) * 2 + jnp.bitwise_xor(at // 8, high)
        lines = pack(grad[64 * u : 64 * u + 64])

        @pl.when(core == u % 2)
        def _():
            own_ref[near] = lines

        @pl.when(core != u % 2)
        def _():
            other_ref[near] = lines


def target_gradients(member, a, q):
    out = jax.ShapeDtypeStruct((8, LINES, 128), jnp.bfloat16)
    whole = pl.BlockSpec((8, LINES, 128), lambda k: (0, 0, 0))
    return pl.pallas_call(
        target_kernel,
        grid=(PART // TILE,),
        in_specs=[
            pl.BlockSpec(memory_space=pltpu.SMEM),
            pl.BlockSpec((NREL, TILE, PART), lambda k: (0, k, 0)),
            pl.BlockSpec((NREL, PART, DIM), lambda k: (0, 0, 0)),
        ],
        out_specs=[whole, whole],
        out_shape=[out, out],
        compiler_params=pltpu.CompilerParams(vmem_limit_bytes=VMEM_LIMIT),
        cost_estimate=pl.CostEstimate(flops=4 << 30, bytes_accessed=12 << 20, transcendentals=0),
        name="target_gradients",
    )(member, a, q)


def update_kernel(part_ref, table_ref, state_ref, new_table_ref, new_state_ref):
    lines = part_ref[0].astype(jnp.float32)
    for k in range(1, part_ref.shape[0]):
        lines = lines + part_ref[k].astype(jnp.float32)
    grad = unpack(lines)
    rows = grad.shape[0]
    mean = jnp.sum(grad * grad, axis=1, keepdims=True) / DIM
    mean_row = jnp.broadcast_to(mean, (rows, 128)).T[:1]
    new_state_row = state_ref[...] + mean_row
    new_state_ref[...] = new_state_row
    new_state = jnp.broadcast_to(new_state_row, (128, rows)).T[:, :1]
    new_table_ref[...] = table_ref[...] - learn_rate * grad / (jnp.sqrt(new_state) + epsilon)


def update(parts, table, state):
    rows = table.shape[0]
    new_table, new_state = pl.pallas_call(
        update_kernel,
        out_shape=[jax.ShapeDtypeStruct(table.shape, jnp.float32), jax.ShapeDtypeStruct((1, rows), jnp.float32)],
        cost_estimate=pl.CostEstimate(flops=1 << 20, bytes_accessed=2 << 20, transcendentals=0),
        name="row_adagrad",
    )(parts, table, state.reshape(1, rows))
    return new_table, new_state.reshape(rows)


HALVES = [(i, i ^ 8) for i in range(16)]
CORES = [(i, i ^ 1) for i in range(16)]


def x_step(k):
    return [(i, (i & 9) | ((((i >> 1) + k) & 3) << 1)) for i in range(16)]


def gather_src(lines):
    near = jnp.stack([lines, lax.ppermute(lines, "src", HALVES)])
    own = jnp.concatenate([near] + [lax.ppermute(near, "src", x_step(k)) for k in (1, 2, 3)])
    return own, lax.ppermute(own, "src", CORES)


def scatter_src(own, other):
    total = own.astype(jnp.float32) + lax.ppermute(other, "src", CORES).astype(jnp.float32)
    sent = total.astype(jnp.bfloat16)
    here = total[:2]
    for k in (1, 2, 3):
        here = here + lax.ppermute(sent[2 * k : 2 * k + 2], "src", x_step(k)).astype(jnp.float32)
    far = lax.ppermute(here[1].astype(jnp.bfloat16), "src", HALVES)
    return jnp.stack([here[0], far.astype(jnp.float32)])


def per_device(
    source_table,
    source_state,
    target_table,
    target_state,
    relations,
    edge_source,
    edge_target,
    batch_relation,
    edge_counts,
    negatives,
):
    member = lax.axis_index("src").reshape(1)
    source_blocks, target_lines = pack_tables(source_table, target_table)
    sources_all = lax.all_to_all(source_blocks, "dst", 0, 0)
    targets_own, targets_other = gather_src(target_lines)
    slots = (1, BATCHES * BATCH)
    n, m = counts(
        batch_relation.reshape(BATCHES),
        edge_counts.reshape(1),
        edge_source.reshape(slots),
        edge_target.reshape(slots),
        negatives.reshape(slots),
    )
    source_grad, a, q = source_gradients(member, sources_all, targets_own, targets_other, relations, n, m)
    source_parts = lax.all_to_all(source_grad, "dst", 0, 0)
    target_parts = scatter_src(*target_gradients(member, a, q))
    new_source_table, new_source_state = update(source_parts, source_table, source_state)
    new_target_table, new_target_state = update(target_parts, target_table, target_state)
    return (new_source_table, new_source_state, new_target_table, new_target_state)


def solution(mesh):
    return jax.shard_map(
        per_device,
        mesh=mesh,
        in_specs=(
            P(("src", "dst"), None),
            P(("src", "dst")),
            P(("dst", "src"), None),
            P(("dst", "src")),
            P(),
            P("src", "dst", None),
            P("src", "dst", None),
            P("src", "dst", None),
            P("src", "dst"),
            P("src", "dst", None, None),
        ),
        out_specs=(
            P(("src", "dst"), None),
            P(("src", "dst")),
            P(("dst", "src"), None),
            P(("dst", "src")),
        ),
        check_vma=False,
    )
```

```python
import jax
import jax.numpy as jnp
from jax import lax
from jax.experimental import pallas as pl
from jax.experimental.pallas import tpu as pltpu
from jax.sharding import PartitionSpec as P

BATCH = 512
NEG = 512
BATCHES = 12
NREL = 4
PART = 1024
DIM = 400
GROUP = 16
LINES = 208
TILE = 1024
COUNT_TILE = 256
ONE_HOT = jnp.float8_e4m3fn

learn_rate = 0.5
epsilon = 1e-08

NT = (((1,), (1,)), ((), ()))
TN = (((0,), (0,)), ((), ()))
COUNT_VMEM = 32 * 1024 * 1024
GRADIENT_VMEM = 48 * 1024 * 1024


def dot(a, b, dims=(((1,), (0,)), ((), ()))):
    return lax.dot_general(a, b, dims, preferred_element_type=jnp.float32)


def one_hot_columns(ids, rows, first, value, dtype):
    row = lax.broadcasted_iota(jnp.int32, (rows, ids.shape[1]), 0) + first
    return jnp.where(row == ids, jnp.float32(value), jnp.float32(0.0)).astype(dtype)


def histogram(ids, value):
    high = one_hot_columns(jnp.right_shift(ids, 7), 8, 0, 1.0, jnp.bfloat16)
    low = one_hot_columns(jnp.bitwise_and(ids, 127), 128, 0, value, jnp.bfloat16)
    table = dot(high, low, NT)
    return jnp.concatenate([table[k : k + 1] for k in range(8)], axis=1)


def count_kernel(rel_ref, cnt_ref, es_ref, et_ref, neg_ref, n_ref, m_ref, ohs, acc, srch, negh):
    step = pl.program_id(0)
    valid = cnt_ref[0]

    def sources_of(b):
        slot = lax.broadcasted_iota(jnp.int32, (1, BATCH), 1) + b * BATCH
        return jnp.where(slot < valid, es_ref[:, b * BATCH : (b + 1) * BATCH], -1)

    @pl.when(step == 0)
    def _():
        for b in range(BATCHES):
            ids = sources_of(b)
            column = jnp.broadcast_to(ids, (128, BATCH)).T[:, :1]
            lane = lax.broadcasted_iota(jnp.int32, (BATCH, PART), 1)
            ohs[b] = jnp.where(lane == column, jnp.float32(1.0), jnp.float32(0.0)).astype(ONE_HOT)
            srch[b : b + 1] = histogram(ids, 1.0)
            negh[b : b + 1] = histogram(neg_ref[:, b * BATCH : (b + 1) * BATCH], 1.0 / 1024.0)
        srch[BATCHES:] = jnp.zeros((16 - BATCHES, PART), jnp.float32)
        negh[BATCHES:] = jnp.zeros((16 - BATCHES, PART), jnp.float32)

    acc[...] = jnp.zeros_like(acc)
    for b in range(BATCHES):
        oht = one_hot_columns(et_ref[:, b * BATCH : (b + 1) * BATCH], COUNT_TILE, step * COUNT_TILE, 0.5, ONE_HOT)
        acc[rel_ref[b]] += dot(oht, ohs[b])

    n_ref[...] = acc[...].astype(jnp.bfloat16)
    lanes = pl.ds(pl.multiple_of(step * COUNT_TILE, COUNT_TILE), COUNT_TILE)
    negs = negh[:, lanes].astype(jnp.bfloat16)
    row = lax.broadcasted_iota(jnp.int32, (16, 1), 0)
    rel = jnp.full((16, 1), -1, jnp.int32)
    for b in range(BATCHES):
        rel = jnp.where(row == b, rel_ref[b], rel)
    for r in range(NREL):
        kept = jnp.where(rel == r, srch[...], 0.0).astype(jnp.bfloat16)
        m_ref[r] = dot(negs, kept, TN).astype(jnp.bfloat16)


def counts(rel, cnt, es, et, neg):
    smem = pl.BlockSpec(memory_space=pltpu.SMEM)
    whole = pl.BlockSpec((1, BATCHES * BATCH), lambda t: (0, 0))
    tiles = pl.BlockSpec((NREL, COUNT_TILE, PART), lambda t: (0, t, 0))
    out = jax.ShapeDtypeStruct((NREL, PART, PART), jnp.bfloat16)
    return pl.pallas_call(
        count_kernel,
        grid=(PART // COUNT_TILE,),
        in_specs=[smem, smem, whole, whole, whole],
        out_specs=[tiles, tiles],
        out_shape=[out, out],
        scratch_shapes=[
            pltpu.VMEM((BATCHES, BATCH, PART), ONE_HOT),
            pltpu.VMEM((NREL, COUNT_TILE, PART), jnp.float32),
            pltpu.VMEM((16, PART), jnp.float32),
            pltpu.VMEM((16, PART), jnp.float32),
        ],
        compiler_params=pltpu.CompilerParams(vmem_limit_bytes=COUNT_VMEM),
        cost_estimate=pl.CostEstimate(flops=2 * PART * PART * BATCHES * BATCH, bytes_accessed=16 << 20, transcendentals=0),
        name="pair_counts",
    )(rel, cnt, es, et, neg)


def pack(block):
    parts = [block[:, 128 * c : 128 * c + 128] for c in range(3)]
    tail = [block[16 * g : 16 * g + 16, 384:DIM] for g in range(4)]
    parts.append(jnp.concatenate(tail + [jnp.zeros((16, 64), block.dtype)], axis=1))
    return jnp.concatenate(parts, axis=0)


def unpack(lines):
    parts = [lines[64 * c : 64 * c + 64] for c in range(3)]
    tail = [lines[192:208, 16 * g : 16 * g + 16] for g in range(4)]
    parts.append(jnp.concatenate(tail, axis=0))
    return jnp.concatenate(parts, axis=1)


def pack_kernel(source_ref, target_ref, spread_ref, packed_ref):
    lines = pack(source_ref[...]).astype(jnp.bfloat16)
    for d in range(GROUP):
        spread_ref[d] = lines
    packed_ref[...] = pack(target_ref[...]).astype(jnp.bfloat16)


def pack_tables(source_table, target_table):
    return pl.pallas_call(
        pack_kernel,
        out_shape=[
            jax.ShapeDtypeStruct((GROUP, LINES, 128), jnp.bfloat16),
            jax.ShapeDtypeStruct((LINES, 128), jnp.bfloat16),
        ],
        name="pack_tables",
    )(source_table, target_table)


def place(member, near, other):
    high, x, core = member // 8, (member // 2) % 4, member % 2
    return jnp.bitwise_xor(high, near % 2) * 8 + ((x + 4 - near // 2) % 4) * 2 + jnp.bitwise_xor(core, other)


def gradient_kernel(
    member_ref, s_ref, t_own_ref, t_other_ref, rel_ref, n_ref, m_ref, gs_ref, own_ref, other_ref,
    s, half, tt, q0, q1, a0, a1, sacc, tacc,
):
    r, k = pl.program_id(0), pl.program_id(1)
    member = member_ref[0]
    high, x, core = member // 8, (member // 2) % 4, member % 2
    tile = pl.ds(pl.multiple_of(k * TILE, TILE), TILE)
    qs, coefs = (q0, q1), (a0, a1)

    @pl.when((r == 0) & (k == 0))
    def _():
        for d in range(GROUP):
            s[64 * d : 64 * d + 64] = unpack(s_ref[d])
        for other, ref in enumerate((t_own_ref, t_other_ref)):
            for near in range(8):
                first = pl.multiple_of(place(member, near, other) * 64, 64)
                half[pl.ds(first, 64)] = unpack(ref[near])
        tt[...] = half[...].astype(jnp.float32).T.astype(jnp.bfloat16)
        half[...] = half[...] * jnp.bfloat16(0.5)
        sacc[...] = jnp.zeros_like(sacc)
        tacc[...] = jnp.zeros_like(tacc)
        q0[...] = dot(s[...], rel_ref[0]).astype(jnp.bfloat16)

    def targets_part(i):
        q = qs[i % 2]
        th = jnp.tanh(dot(half[tile], q[...], NT))
        coef = n_ref[0].astype(jnp.float32) * (th - 1.0) + m_ref[0].astype(jnp.float32) * (th + 1.0)
        coef = coef.astype(jnp.bfloat16)
        coefs[i % 2][tile] = coef
        if i + 1 < NREL:
            qs[(i + 1) % 2][tile] = dot(s[tile], rel_ref[i + 1]).astype(jnp.bfloat16)
        grad = tacc[tile] + dot(coef, q[...])
        if i + 1 < NREL:
            tacc[tile] = grad
            return
        grad = grad.astype(jnp.bfloat16)
        for u in range(TILE // 64):
            at = k * (TILE // 64) + u
            near = (((at // 2) % 4 + 4 - x) % 4) * 2 + jnp.bitwise_xor(at // 8, high)
            lines = pack(grad[64 * u : 64 * u + 64])

            @pl.when(core == u % 2)
            def _():
                own_ref[near] = lines

            @pl.when(core != u % 2)
            def _():
                other_ref[near] = lines

    def sources_part(i):
        query_grad = dot(tt[...], coefs[i % 2][:, tile]).astype(jnp.bfloat16)
        grad = sacc[:, tile] + dot(rel_ref[i], query_grad)
        if i + 1 < NREL:
            sacc[:, tile] = grad
            return
        grad = grad.T.astype(jnp.bfloat16)
        for u in range(TILE // 64):
            gs_ref[k * (TILE // 64) + u] = pack(grad[64 * u : 64 * u + 64])

    for i in range(NREL + 1):

        @pl.when(r == i)
        def _():
            if i > 0:
                sources_part(i - 1)
            if i < NREL:
                targets_part(i)


def gradients(member, sources, targets_own, targets_other, relations, n, m):
    tiles = pl.BlockSpec(
        (1, TILE, PART),
        lambda r, k: (jnp.minimum(r, NREL - 1), jnp.where(r == NREL, PART // TILE - 1, k), 0),
    )

    def blocks(count):
        return pl.BlockSpec((count, LINES, 128), lambda r, k: (0, 0, 0))

    wide = pltpu.VMEM((PART, DIM), jnp.bfloat16)
    square = pltpu.VMEM((PART, PART), jnp.bfloat16)
    return pl.pallas_call(
        gradient_kernel,
        grid=(NREL + 1, PART // TILE),
        in_specs=[
            pl.BlockSpec(memory_space=pltpu.SMEM),
            blocks(GROUP),
            blocks(8),
            blocks(8),
            pl.BlockSpec((NREL, DIM, DIM), lambda r, k: (0, 0, 0)),
            tiles,
            tiles,
        ],
        out_specs=[blocks(GROUP), blocks(8), blocks(8)],
        out_shape=[
            jax.ShapeDtypeStruct((GROUP, LINES, 128), jnp.bfloat16),
            jax.ShapeDtypeStruct((8, LINES, 128), jnp.bfloat16),
            jax.ShapeDtypeStruct((8, LINES, 128), jnp.bfloat16),
        ],
        scratch_shapes=[
            wide,
            wide,
            pltpu.VMEM((DIM, PART), jnp.bfloat16),
            wide,
            wide,
            square,
            square,
            pltpu.VMEM((DIM, PART), jnp.float32),
            pltpu.VMEM((PART, DIM), jnp.float32),
        ],
        compiler_params=pltpu.CompilerParams(vmem_limit_bytes=GRADIENT_VMEM),
        cost_estimate=pl.CostEstimate(flops=16 << 30, bytes_accessed=20 << 20, transcendentals=4 << 20),
        name="gradients",
    )(member, sources, targets_own, targets_other, relations, n, m)


def update_kernel(part_ref, table_ref, state_ref, new_table_ref, new_state_ref):
    lines = part_ref[0].astype(jnp.float32)
    for k in range(1, part_ref.shape[0]):
        lines = lines + part_ref[k].astype(jnp.float32)
    grad = unpack(lines)
    rows = grad.shape[0]
    mean = jnp.sum(grad * grad, axis=1, keepdims=True) / DIM
    mean_row = jnp.broadcast_to(mean, (rows, 128)).T[:1]
    new_state_row = state_ref[...] + mean_row
    new_state_ref[...] = new_state_row
    new_state = jnp.broadcast_to(new_state_row, (128, rows)).T[:, :1]
    new_table_ref[...] = table_ref[...] - learn_rate * grad / (jnp.sqrt(new_state) + epsilon)


def update(parts, table, state):
    rows = table.shape[0]
    new_table, new_state = pl.pallas_call(
        update_kernel,
        out_shape=[jax.ShapeDtypeStruct(table.shape, jnp.float32), jax.ShapeDtypeStruct((1, rows), jnp.float32)],
        cost_estimate=pl.CostEstimate(flops=1 << 20, bytes_accessed=2 << 20, transcendentals=0),
        name="row_adagrad",
    )(parts, table, state.reshape(1, rows))
    return new_table, new_state.reshape(rows)


HALVES = [(i, i ^ 8) for i in range(16)]
CORES = [(i, i ^ 1) for i in range(16)]


def x_step(k):
    return [(i, (i & 9) | ((((i >> 1) + k) & 3) << 1)) for i in range(16)]


def gather_src(lines):
    near = jnp.stack([lines, lax.ppermute(lines, "src", HALVES)])
    own = jnp.concatenate([near] + [lax.ppermute(near, "src", x_step(k)) for k in (1, 2, 3)])
    return own, lax.ppermute(own, "src", CORES)


def scatter_src(own, other):
    total = own.astype(jnp.float32) + lax.ppermute(other, "src", CORES).astype(jnp.float32)
    sent = total.astype(jnp.bfloat16)
    here = total[:2]
    for k in (1, 2, 3):
        here = here + lax.ppermute(sent[2 * k : 2 * k + 2], "src", x_step(k)).astype(jnp.float32)
    far = lax.ppermute(here[1].astype(jnp.bfloat16), "src", HALVES)
    return jnp.stack([here[0], far.astype(jnp.float32)])


def per_device(
    source_table,
    source_state,
    target_table,
    target_state,
    relations,
    edge_source,
    edge_target,
    batch_relation,
    edge_counts,
    negatives,
):
    member = lax.axis_index("src").reshape(1)
    source_blocks, target_lines = pack_tables(source_table, target_table)
    sources_all = lax.all_to_all(source_blocks, "dst", 0, 0)
    targets_own, targets_other = gather_src(target_lines)
    slots = (1, BATCHES * BATCH)
    n, m = counts(
        batch_relation.reshape(BATCHES),
        edge_counts.reshape(1),
        edge_source.reshape(slots),
        edge_target.reshape(slots),
        negatives.reshape(slots),
    )
    source_grad, own, other = gradients(member, sources_all, targets_own, targets_other, relations, n, m)
    source_parts = lax.all_to_all(source_grad, "dst", 0, 0)
    target_parts = scatter_src(own, other)
    new_source_table, new_source_state = update(source_parts, source_table, source_state)
    new_target_table, new_target_state = update(target_parts, target_table, target_state)
    return (new_source_table, new_source_state, new_target_table, new_target_state)


def solution(mesh):
    return jax.shard_map(
        per_device,
        mesh=mesh,
        in_specs=(
            P(("src", "dst"), None),
            P(("src", "dst")),
            P(("dst", "src"), None),
            P(("dst", "src")),
            P(),
            P("src", "dst", None),
            P("src", "dst", None),
            P("src", "dst", None),
            P("src", "dst"),
            P("src", "dst", None, None),
        ),
        out_specs=(
            P(("src", "dst"), None),
            P(("src", "dst")),
            P(("dst", "src"), None),
            P(("dst", "src")),
        ),
        check_vma=False,
    )
```

```python
import jax
import jax.numpy as jnp
from jax import lax
from jax.experimental import pallas as pl
from jax.experimental.pallas import tpu as pltpu
from jax.sharding import PartitionSpec as P

BATCH = 512
NEG = 512
BATCHES = 12
NREL = 4
PART = 1024
DIM = 400
GROUP = 16
LINES = 208
TILE = 1024
COUNT_TILE = 256
ONE_HOT = jnp.float8_e4m3fn

learn_rate = 0.5
epsilon = 1e-08

NT = (((1,), (1,)), ((), ()))
TN = (((0,), (0,)), ((), ()))
COUNT_VMEM = 56 * 1024 * 1024
UPDATE_VMEM = 8 * 1024 * 1024
GRADIENT_VMEM = 48 * 1024 * 1024


def dot(a, b, dims=(((1,), (0,)), ((), ()))):
    return lax.dot_general(a, b, dims, preferred_element_type=jnp.float32)


def one_hot_columns(ids, rows, first, value, dtype):
    row = lax.broadcasted_iota(jnp.int32, (rows, ids.shape[1]), 0) + first
    return jnp.where(row == ids, jnp.float32(value), jnp.float32(0.0)).astype(dtype)


def histogram(ids, value):
    high = one_hot_columns(jnp.right_shift(ids, 7), 8, 0, 1.0, jnp.bfloat16)
    low = one_hot_columns(jnp.bitwise_and(ids, 127), 128, 0, value, jnp.bfloat16)
    table = dot(high, low, NT)
    return jnp.concatenate([table[k : k + 1] for k in range(8)], axis=1)


def count_kernel(rel_ref, cnt_ref, es_ref, et_ref, neg_ref, n_ref, m_ref, ohs, acc, srch, negh):
    step = pl.program_id(0)
    valid = cnt_ref[0]

    def sources_of(b):
        slot = lax.broadcasted_iota(jnp.int32, (1, BATCH), 1) + b * BATCH
        return jnp.where(slot < valid, es_ref[:, b * BATCH : (b + 1) * BATCH], -1)

    @pl.when(step == 0)
    def _():
        for b in range(BATCHES):
            ids = sources_of(b)
            column = jnp.broadcast_to(ids, (128, BATCH)).T[:, :1]
            lane = lax.broadcasted_iota(jnp.int32, (BATCH, PART), 1)
            ohs[b] = jnp.where(lane == column, jnp.float32(1.0), jnp.float32(0.0)).astype(ONE_HOT)
            srch[b : b + 1] = histogram(ids, 1.0)
            negh[b : b + 1] = histogram(neg_ref[:, b * BATCH : (b + 1) * BATCH], 1.0 / 1024.0)
        srch[BATCHES:] = jnp.zeros((16 - BATCHES, PART), jnp.float32)
        negh[BATCHES:] = jnp.zeros((16 - BATCHES, PART), jnp.float32)

    acc[...] = jnp.zeros_like(acc)
    for b in range(BATCHES):
        oht = one_hot_columns(et_ref[:, b * BATCH : (b + 1) * BATCH], COUNT_TILE, step * COUNT_TILE, 0.5, ONE_HOT)
        acc[rel_ref[b]] += dot(oht, ohs[b])

    n_ref[...] = acc[...].astype(jnp.bfloat16)
    lanes = pl.ds(pl.multiple_of(step * COUNT_TILE, COUNT_TILE), COUNT_TILE)
    negs = negh[:, lanes].astype(jnp.bfloat16)
    row = lax.broadcasted_iota(jnp.int32, (16, 1), 0)
    rel = jnp.full((16, 1), -1, jnp.int32)
    for b in range(BATCHES):
        rel = jnp.where(row == b, rel_ref[b], rel)
    for r in range(NREL):
        kept = jnp.where(rel == r, srch[...], 0.0).astype(jnp.bfloat16)
        m_ref[r] = dot(negs, kept, TN).astype(jnp.bfloat16)


def counts(rel, cnt, es, et, neg):
    smem = pl.BlockSpec(memory_space=pltpu.SMEM)
    whole = pl.BlockSpec((1, BATCHES * BATCH), lambda t: (0, 0))
    tiles = pl.BlockSpec((NREL, COUNT_TILE, PART), lambda t: (0, t, 0))
    out = jax.ShapeDtypeStruct((NREL, PART, PART), jnp.bfloat16)
    return pl.pallas_call(
        count_kernel,
        grid=(PART // COUNT_TILE,),
        in_specs=[smem, smem, whole, whole, whole],
        out_specs=[tiles, tiles],
        out_shape=[out, out],
        scratch_shapes=[
            pltpu.VMEM((BATCHES, BATCH, PART), ONE_HOT),
            pltpu.VMEM((NREL, COUNT_TILE, PART), jnp.float32),
            pltpu.VMEM((16, PART), jnp.float32),
            pltpu.VMEM((16, PART), jnp.float32),
        ],
        compiler_params=pltpu.CompilerParams(vmem_limit_bytes=COUNT_VMEM),
        cost_estimate=pl.CostEstimate(flops=2 * PART * PART * BATCHES * BATCH, bytes_accessed=16 << 20, transcendentals=0),
        name="pair_counts",
    )(rel, cnt, es, et, neg)


def pack(block):
    parts = [block[:, 128 * c : 128 * c + 128] for c in range(3)]
    tail = [block[16 * g : 16 * g + 16, 384:DIM] for g in range(4)]
    parts.append(jnp.concatenate(tail + [jnp.zeros((16, 64), block.dtype)], axis=1))
    return jnp.concatenate(parts, axis=0)


def unpack(lines):
    parts = [lines[64 * c : 64 * c + 64] for c in range(3)]
    tail = [lines[192:208, 16 * g : 16 * g + 16] for g in range(4)]
    parts.append(jnp.concatenate(tail, axis=0))
    return jnp.concatenate(parts, axis=1)


def pack_kernel(source_ref, target_ref, spread_ref, packed_ref):
    lines = pack(source_ref[...]).astype(jnp.bfloat16)
    for d in range(GROUP):
        spread_ref[d] = lines
    packed_ref[...] = pack(target_ref[...]).astype(jnp.bfloat16)


def pack_tables(source_table, target_table):
    return pl.pallas_call(
        pack_kernel,
        out_shape=[
            jax.ShapeDtypeStruct((GROUP, LINES, 128), jnp.bfloat16),
            jax.ShapeDtypeStruct((LINES, 128), jnp.bfloat16),
        ],
        name="pack_tables",
    )(source_table, target_table)


def place(member, near, other):
    high, x, core = member // 8, (member // 2) % 4, member % 2
    return jnp.bitwise_xor(high, near % 2) * 8 + ((x + 4 - near // 2) % 4) * 2 + jnp.bitwise_xor(core, other)


def gradient_kernel(
    member_ref, s_ref, t_own_ref, t_other_ref, rel_ref, n_ref, m_ref, gs_ref, own_ref, other_ref,
    s, half, tt, q0, q1, a0, a1, sacc, tacc,
):
    r, k = pl.program_id(0), pl.program_id(1)
    member = member_ref[0]
    high, x, core = member // 8, (member // 2) % 4, member % 2
    tile = pl.ds(pl.multiple_of(k * TILE, TILE), TILE)
    qs, coefs = (q0, q1), (a0, a1)

    @pl.when((r == 0) & (k == 0))
    def _():
        for d in range(GROUP):
            s[64 * d : 64 * d + 64] = unpack(s_ref[d])
        for other, ref in enumerate((t_own_ref, t_other_ref)):
            for near in range(8):
                first = pl.multiple_of(place(member, near, other) * 64, 64)
                half[pl.ds(first, 64)] = unpack(ref[near])
        tt[...] = half[...].astype(jnp.float32).T.astype(jnp.bfloat16)
        half[...] = half[...] * jnp.bfloat16(0.5)
        sacc[...] = jnp.zeros_like(sacc)
        tacc[...] = jnp.zeros_like(tacc)
        q0[...] = dot(s[...], rel_ref[0]).astype(jnp.bfloat16)

    def targets_part(i):
        q = qs[i % 2]
        th = jnp.tanh(dot(half[tile], q[...], NT))
        coef = n_ref[0].astype(jnp.float32) * (th - 1.0) + m_ref[0].astype(jnp.float32) * (th + 1.0)
        coef = coef.astype(jnp.bfloat16)
        coefs[i % 2][tile] = coef
        if i + 1 < NREL:
            qs[(i + 1) % 2][tile] = dot(s[tile], rel_ref[i + 1]).astype(jnp.bfloat16)
        grad = tacc[tile] + dot(coef, q[...])
        if i + 1 < NREL:
            tacc[tile] = grad
            return
        grad = grad.astype(jnp.bfloat16)
        for u in range(TILE // 64):
            at = k * (TILE // 64) + u
            near = (((at // 2) % 4 + 4 - x) % 4) * 2 + jnp.bitwise_xor(at // 8, high)
            lines = pack(grad[64 * u : 64 * u + 64])

            @pl.when(core == u % 2)
            def _():
                own_ref[near] = lines

            @pl.when(core != u % 2)
            def _():
                other_ref[near] = lines

    def sources_part(i):
        query_grad = dot(tt[...], coefs[i % 2][:, tile]).astype(jnp.bfloat16)
        grad = sacc[:, tile] + dot(rel_ref[i], query_grad)
        if i + 1 < NREL:
            sacc[:, tile] = grad
            return
        grad = grad.T.astype(jnp.bfloat16)
        for u in range(TILE // 64):
            gs_ref[k * (TILE // 64) + u] = pack(grad[64 * u : 64 * u + 64])

    for i in range(NREL + 1):

        @pl.when(r == i)
        def _():
            if i > 0:
                sources_part(i - 1)
            if i < NREL:
                targets_part(i)


def gradients(member, sources, targets_own, targets_other, relations, n, m):
    tiles = pl.BlockSpec(
        (1, TILE, PART),
        lambda r, k: (jnp.minimum(r, NREL - 1), jnp.where(r == NREL, PART // TILE - 1, k), 0),
    )

    def blocks(count):
        return pl.BlockSpec((count, LINES, 128), lambda r, k: (0, 0, 0))

    wide = pltpu.VMEM((PART, DIM), jnp.bfloat16)
    square = pltpu.VMEM((PART, PART), jnp.bfloat16)
    return pl.pallas_call(
        gradient_kernel,
        grid=(NREL + 1, PART // TILE),
        in_specs=[
            pl.BlockSpec(memory_space=pltpu.SMEM),
            blocks(GROUP),
            blocks(8),
            blocks(8),
            pl.BlockSpec((NREL, DIM, DIM), lambda r, k: (0, 0, 0)),
            tiles,
            tiles,
        ],
        out_specs=[blocks(GROUP), blocks(8), blocks(8)],
        out_shape=[
            jax.ShapeDtypeStruct((GROUP, LINES, 128), jnp.bfloat16),
            jax.ShapeDtypeStruct((8, LINES, 128), jnp.bfloat16),
            jax.ShapeDtypeStruct((8, LINES, 128), jnp.bfloat16),
        ],
        scratch_shapes=[
            wide,
            wide,
            pltpu.VMEM((DIM, PART), jnp.bfloat16),
            wide,
            wide,
            square,
            square,
            pltpu.VMEM((DIM, PART), jnp.float32),
            pltpu.VMEM((PART, DIM), jnp.float32),
        ],
        compiler_params=pltpu.CompilerParams(vmem_limit_bytes=GRADIENT_VMEM),
        cost_estimate=pl.CostEstimate(flops=16 << 30, bytes_accessed=20 << 20, transcendentals=4 << 20),
        name="gradients",
    )(member, sources, targets_own, targets_other, relations, n, m)


def update_kernel(part_ref, table_ref, state_ref, new_table_ref, new_state_ref):
    lines = part_ref[0].astype(jnp.float32)
    for k in range(1, part_ref.shape[0]):
        lines = lines + part_ref[k].astype(jnp.float32)
    grad = unpack(lines)
    rows = grad.shape[0]
    mean = jnp.sum(grad * grad, axis=1, keepdims=True) / DIM
    mean_row = jnp.broadcast_to(mean, (rows, 128)).T[:1]
    new_state_row = state_ref[...] + mean_row
    new_state_ref[...] = new_state_row
    new_state = jnp.broadcast_to(new_state_row, (128, rows)).T[:, :1]
    new_table_ref[...] = table_ref[...] - learn_rate * grad / (jnp.sqrt(new_state) + epsilon)


def update(parts, table, state):
    rows = table.shape[0]
    new_table, new_state = pl.pallas_call(
        update_kernel,
        out_shape=[jax.ShapeDtypeStruct(table.shape, jnp.float32), jax.ShapeDtypeStruct((1, rows), jnp.float32)],
        compiler_params=pltpu.CompilerParams(vmem_limit_bytes=UPDATE_VMEM),
        cost_estimate=pl.CostEstimate(flops=1 << 20, bytes_accessed=2 << 20, transcendentals=0),
        name="row_adagrad",
    )(parts, table, state.reshape(1, rows))
    return new_table, new_state.reshape(rows)


HALVES = [(i, i ^ 8) for i in range(16)]
CORES = [(i, i ^ 1) for i in range(16)]


def x_step(k):
    return [(i, (i & 9) | ((((i >> 1) + k) & 3) << 1)) for i in range(16)]


def gather_src(lines, beside, operands):
    near = jnp.stack([lines, lax.ppermute(lines, "src", HALVES)])
    near, operands = lax.optimization_barrier((near, operands))
    results = beside(*operands)
    own = jnp.concatenate([near] + [lax.ppermute(near, "src", x_step(k)) for k in (1, 2, 3)])
    own, results = lax.optimization_barrier((own, results))
    return own, lax.ppermute(own, "src", CORES), results


def scatter_src(own, other):
    total = own.astype(jnp.float32) + lax.ppermute(other, "src", CORES).astype(jnp.float32)
    sent = total.astype(jnp.bfloat16)
    here = total[:2]
    for k in (1, 2, 3):
        here = here + lax.ppermute(sent[2 * k : 2 * k + 2], "src", x_step(k)).astype(jnp.float32)
    far = lax.ppermute(here[1].astype(jnp.bfloat16), "src", HALVES)
    return jnp.stack([here[0], far.astype(jnp.float32)])


def per_device(
    source_table,
    source_state,
    target_table,
    target_state,
    relations,
    edge_source,
    edge_target,
    batch_relation,
    edge_counts,
    negatives,
):
    member = lax.axis_index("src").reshape(1)
    source_blocks, target_lines = pack_tables(source_table, target_table)
    sources_all = lax.all_to_all(source_blocks, "dst", 0, 0)
    slots = (1, BATCHES * BATCH)
    lists = (
        batch_relation.reshape(BATCHES),
        edge_counts.reshape(1),
        edge_source.reshape(slots),
        edge_target.reshape(slots),
        negatives.reshape(slots),
    )
    targets_own, targets_other, (n, m) = gather_src(target_lines, counts, lists)
    source_grad, own, other = gradients(member, sources_all, targets_own, targets_other, relations, n, m)
    source_parts = lax.all_to_all(source_grad, "dst", 0, 0)
    target_parts = scatter_src(own, other)
    new_source_table, new_source_state = update(source_parts, source_table, source_state)
    new_target_table, new_target_state = update(target_parts, target_table, target_state)
    return (new_source_table, new_source_state, new_target_table, new_target_state)


def solution(mesh):
    return jax.shard_map(
        per_device,
        mesh=mesh,
        in_specs=(
            P(("src", "dst"), None),
            P(("src", "dst")),
            P(("dst", "src"), None),
            P(("dst", "src")),
            P(),
            P("src", "dst", None),
            P("src", "dst", None),
            P("src", "dst", None),
            P("src", "dst"),
            P("src", "dst", None, None),
        ),
        out_specs=(
            P(("src", "dst"), None),
            P(("src", "dst")),
            P(("dst", "src"), None),
            P(("dst", "src")),
        ),
        check_vma=False,
    )
```

```python
import jax
import jax.numpy as jnp
from jax import lax
from jax.experimental import pallas as pl
from jax.experimental.pallas import tpu as pltpu
from jax.sharding import PartitionSpec as P

BATCH = 512
NEG = 512
BATCHES = 12
NREL = 4
PART = 1024
DIM = 400
GROUP = 16
LINES = 208
TILE = 1024
COUNT_TILE = 256
ONE_HOT = jnp.float8_e4m3fn

learn_rate = 0.5
epsilon = 1e-08

NT = (((1,), (1,)), ((), ()))
TN = (((0,), (0,)), ((), ()))
COUNT_VMEM = 56 * 1024 * 1024
UPDATE_VMEM = 8 * 1024 * 1024
GRADIENT_VMEM = 48 * 1024 * 1024


def dot(a, b, dims=(((1,), (0,)), ((), ()))):
    return lax.dot_general(a, b, dims, preferred_element_type=jnp.float32)


def one_hot_columns(ids, rows, first, value, dtype):
    row = lax.broadcasted_iota(jnp.int32, (rows, ids.shape[1]), 0) + first
    return jnp.where(row == ids, jnp.float32(value), jnp.float32(0.0)).astype(dtype)


def histogram(ids, value):
    high = one_hot_columns(jnp.right_shift(ids, 7), 8, 0, 1.0, jnp.bfloat16)
    low = one_hot_columns(jnp.bitwise_and(ids, 127), 128, 0, value, jnp.bfloat16)
    table = dot(high, low, NT)
    return jnp.concatenate([table[k : k + 1] for k in range(8)], axis=1)


def count_kernel(rel_ref, cnt_ref, es_ref, et_ref, neg_ref, n_ref, m_ref, ohs, acc, srch, negh):
    step = pl.program_id(0)
    valid = cnt_ref[0]

    def sources_of(b):
        slot = lax.broadcasted_iota(jnp.int32, (1, BATCH), 1) + b * BATCH
        return jnp.where(slot < valid, es_ref[:, b * BATCH : (b + 1) * BATCH], -1)

    @pl.when(step == 0)
    def _():
        for b in range(BATCHES):
            ids = sources_of(b)
            column = jnp.broadcast_to(ids, (128, BATCH)).T[:, :1]
            lane = lax.broadcasted_iota(jnp.int32, (BATCH, PART), 1)
            ohs[b] = jnp.where(lane == column, jnp.float32(1.0), jnp.float32(0.0)).astype(ONE_HOT)
            srch[b : b + 1] = histogram(ids, 1.0)
            negh[b : b + 1] = histogram(neg_ref[:, b * BATCH : (b + 1) * BATCH], 1.0 / 1024.0)
        srch[BATCHES:] = jnp.zeros((16 - BATCHES, PART), jnp.float32)
        negh[BATCHES:] = jnp.zeros((16 - BATCHES, PART), jnp.float32)

    for r in range(NREL):
        uses = jnp.int32(0)
        for b in range(BATCHES):
            uses = uses + (rel_ref[b] == r).astype(jnp.int32)

        @pl.when(uses == 0)
        def _():
            acc[r] = jnp.zeros((COUNT_TILE, PART), jnp.float32)

    for b in range(BATCHES):
        oht = one_hot_columns(et_ref[:, b * BATCH : (b + 1) * BATCH], COUNT_TILE, step * COUNT_TILE, 0.5, ONE_HOT)
        r = rel_ref[b]
        seen = jnp.int32(0)
        for c in range(b):
            seen = seen + (rel_ref[c] == r).astype(jnp.int32)
        acc[r] = jnp.where(seen > 0, acc[r], 0.0) + dot(oht, ohs[b])

    n_ref[...] = acc[...].astype(jnp.bfloat16)
    lanes = pl.ds(pl.multiple_of(step * COUNT_TILE, COUNT_TILE), COUNT_TILE)
    negs = negh[:, lanes].astype(jnp.bfloat16)
    row = lax.broadcasted_iota(jnp.int32, (16, 1), 0)
    rel = jnp.full((16, 1), -1, jnp.int32)
    for b in range(BATCHES):
        rel = jnp.where(row == b, rel_ref[b], rel)
    for r in range(NREL):
        kept = jnp.where(rel == r, srch[...], 0.0).astype(jnp.bfloat16)
        m_ref[r] = dot(negs, kept, TN).astype(jnp.bfloat16)


def counts(rel, cnt, es, et, neg):
    smem = pl.BlockSpec(memory_space=pltpu.SMEM)
    whole = pl.BlockSpec((1, BATCHES * BATCH), lambda t: (0, 0))
    tiles = pl.BlockSpec((NREL, COUNT_TILE, PART), lambda t: (0, t, 0))
    out = jax.ShapeDtypeStruct((NREL, PART, PART), jnp.bfloat16)
    return pl.pallas_call(
        count_kernel,
        grid=(PART // COUNT_TILE,),
        in_specs=[smem, smem, whole, whole, whole],
        out_specs=[tiles, tiles],
        out_shape=[out, out],
        scratch_shapes=[
            pltpu.VMEM((BATCHES, BATCH, PART), ONE_HOT),
            pltpu.VMEM((NREL, COUNT_TILE, PART), jnp.float32),
            pltpu.VMEM((16, PART), jnp.float32),
            pltpu.VMEM((16, PART), jnp.float32),
        ],
        compiler_params=pltpu.CompilerParams(vmem_limit_bytes=COUNT_VMEM),
        cost_estimate=pl.CostEstimate(flops=2 * PART * PART * BATCHES * BATCH, bytes_accessed=16 << 20, transcendentals=0),
        name="pair_counts",
    )(rel, cnt, es, et, neg)


def pack(block):
    parts = [block[:, 128 * c : 128 * c + 128] for c in range(3)]
    tail = [block[16 * g : 16 * g + 16, 384:DIM] for g in range(4)]
    parts.append(jnp.concatenate(tail + [jnp.zeros((16, 64), block.dtype)], axis=1))
    return jnp.concatenate(parts, axis=0)


def unpack(lines):
    parts = [lines[64 * c : 64 * c + 64] for c in range(3)]
    tail = [lines[192:208, 16 * g : 16 * g + 16] for g in range(4)]
    parts.append(jnp.concatenate(tail, axis=0))
    return jnp.concatenate(parts, axis=1)


def pack_kernel(source_ref, target_ref, spread_ref, packed_ref):
    lines = pack(source_ref[...]).astype(jnp.bfloat16)
    for d in range(GROUP):
        spread_ref[d] = lines
    packed_ref[...] = pack(target_ref[...]).astype(jnp.bfloat16)


def pack_tables(source_table, target_table):
    return pl.pallas_call(
        pack_kernel,
        out_shape=[
            jax.ShapeDtypeStruct((GROUP, LINES, 128), jnp.bfloat16),
            jax.ShapeDtypeStruct((LINES, 128), jnp.bfloat16),
        ],
        name="pack_tables",
    )(source_table, target_table)


def place(member, near, other):
    high, x, core = member // 8, (member // 2) % 4, member % 2
    return jnp.bitwise_xor(high, near % 2) * 8 + ((x + 4 - near // 2) % 4) * 2 + jnp.bitwise_xor(core, other)


def gradient_kernel(
    member_ref, s_ref, t_own_ref, t_other_ref, rel_ref, n_ref, m_ref, gs_ref, own_ref, other_ref,
    s, half, tt, q0, q1, a0, a1, sacc, tacc,
):
    r, k = pl.program_id(0), pl.program_id(1)
    member = member_ref[0]
    high, x, core = member // 8, (member // 2) % 4, member % 2
    tile = pl.ds(pl.multiple_of(k * TILE, TILE), TILE)
    qs, coefs = (q0, q1), (a0, a1)

    @pl.when((r == 0) & (k == 0))
    def _():
        for d in range(GROUP):
            s[64 * d : 64 * d + 64] = unpack(s_ref[d])
        for other, ref in enumerate((t_own_ref, t_other_ref)):
            for near in range(8):
                first = pl.multiple_of(place(member, near, other) * 64, 64)
                half[pl.ds(first, 64)] = unpack(ref[near])
        tt[...] = half[...].astype(jnp.float32).T.astype(jnp.bfloat16)
        half[...] = half[...] * jnp.bfloat16(0.5)
        sacc[...] = jnp.zeros_like(sacc)
        tacc[...] = jnp.zeros_like(tacc)
        q0[...] = dot(s[...], rel_ref[0]).astype(jnp.bfloat16)

    def targets_part(i):
        q = qs[i % 2]
        th = jnp.tanh(dot(half[tile], q[...], NT))
        coef = n_ref[0].astype(jnp.float32) * (th - 1.0) + m_ref[0].astype(jnp.float32) * (th + 1.0)
        coef = coef.astype(jnp.bfloat16)
        coefs[i % 2][tile] = coef
        if i + 1 < NREL:
            qs[(i + 1) % 2][tile] = dot(s[tile], rel_ref[i + 1]).astype(jnp.bfloat16)
        grad = tacc[tile] + dot(coef, q[...])
        if i + 1 < NREL:
            tacc[tile] = grad
            return
        grad = grad.astype(jnp.bfloat16)
        for u in range(TILE // 64):
            at = k * (TILE // 64) + u
            near = (((at // 2) % 4 + 4 - x) % 4) * 2 + jnp.bitwise_xor(at // 8, high)
            lines = pack(grad[64 * u : 64 * u + 64])

            @pl.when(core == u % 2)
            def _():
                own_ref[near] = lines

            @pl.when(core != u % 2)
            def _():
                other_ref[near] = lines

    def sources_part(i):
        query_grad = dot(tt[...], coefs[i % 2][:, tile]).astype(jnp.bfloat16)
        grad = sacc[:, tile] + dot(rel_ref[i], query_grad)
        if i + 1 < NREL:
            sacc[:, tile] = grad
            return
        grad = grad.T.astype(jnp.bfloat16)
        for u in range(TILE // 64):
            gs_ref[k * (TILE // 64) + u] = pack(grad[64 * u : 64 * u + 64])

    for i in range(NREL + 1):

        @pl.when(r == i)
        def _():
            if i > 0:
                sources_part(i - 1)
            if i < NREL:
                targets_part(i)


def gradients(member, sources, targets_own, targets_other, relations, n, m):
    tiles = pl.BlockSpec(
        (1, TILE, PART),
        lambda r, k: (jnp.minimum(r, NREL - 1), jnp.where(r == NREL, PART // TILE - 1, k), 0),
    )

    def blocks(count):
        return pl.BlockSpec((count, LINES, 128), lambda r, k: (0, 0, 0))

    wide = pltpu.VMEM((PART, DIM), jnp.bfloat16)
    square = pltpu.VMEM((PART, PART), jnp.bfloat16)
    return pl.pallas_call(
        gradient_kernel,
        grid=(NREL + 1, PART // TILE),
        in_specs=[
            pl.BlockSpec(memory_space=pltpu.SMEM),
            blocks(GROUP),
            blocks(8),
            blocks(8),
            pl.BlockSpec((NREL, DIM, DIM), lambda r, k: (0, 0, 0)),
            tiles,
            tiles,
        ],
        out_specs=[blocks(GROUP), blocks(8), blocks(8)],
        out_shape=[
            jax.ShapeDtypeStruct((GROUP, LINES, 128), jnp.bfloat16),
            jax.ShapeDtypeStruct((8, LINES, 128), jnp.bfloat16),
            jax.ShapeDtypeStruct((8, LINES, 128), jnp.bfloat16),
        ],
        scratch_shapes=[
            wide,
            wide,
            pltpu.VMEM((DIM, PART), jnp.bfloat16),
            wide,
            wide,
            square,
            square,
            pltpu.VMEM((DIM, PART), jnp.float32),
            pltpu.VMEM((PART, DIM), jnp.float32),
        ],
        compiler_params=pltpu.CompilerParams(vmem_limit_bytes=GRADIENT_VMEM),
        cost_estimate=pl.CostEstimate(flops=16 << 30, bytes_accessed=20 << 20, transcendentals=4 << 20),
        name="gradients",
    )(member, sources, targets_own, targets_other, relations, n, m)


def update_kernel(part_ref, table_ref, state_ref, new_table_ref, new_state_ref):
    lines = part_ref[0].astype(jnp.float32)
    for k in range(1, part_ref.shape[0]):
        lines = lines + part_ref[k].astype(jnp.float32)
    grad = unpack(lines)
    rows = grad.shape[0]
    mean = jnp.sum(grad * grad, axis=1, keepdims=True) / DIM
    mean_row = jnp.broadcast_to(mean, (rows, 128)).T[:1]
    new_state_row = state_ref[...] + mean_row
    new_state_ref[...] = new_state_row
    new_state = jnp.broadcast_to(new_state_row, (128, rows)).T[:, :1]
    new_table_ref[...] = table_ref[...] - learn_rate * grad / (jnp.sqrt(new_state) + epsilon)


def update(parts, table, state):
    rows = table.shape[0]
    new_table, new_state = pl.pallas_call(
        update_kernel,
        out_shape=[jax.ShapeDtypeStruct(table.shape, jnp.float32), jax.ShapeDtypeStruct((1, rows), jnp.float32)],
        compiler_params=pltpu.CompilerParams(vmem_limit_bytes=UPDATE_VMEM),
        cost_estimate=pl.CostEstimate(flops=1 << 20, bytes_accessed=2 << 20, transcendentals=0),
        name="row_adagrad",
    )(parts, table, state.reshape(1, rows))
    return new_table, new_state.reshape(rows)


HALVES = [(i, i ^ 8) for i in range(16)]
CORES = [(i, i ^ 1) for i in range(16)]


def x_step(k):
    return [(i, (i & 9) | ((((i >> 1) + k) & 3) << 1)) for i in range(16)]


def gather_src(lines, beside, operands):
    near = jnp.stack([lines, lax.ppermute(lines, "src", HALVES)])
    near, operands = lax.optimization_barrier((near, operands))
    results = beside(*operands)
    own = jnp.concatenate([near] + [lax.ppermute(near, "src", x_step(k)) for k in (1, 2, 3)])
    own, results = lax.optimization_barrier((own, results))
    return own, lax.ppermute(own, "src", CORES), results


def scatter_src(own, other):
    total = own.astype(jnp.float32) + lax.ppermute(other, "src", CORES).astype(jnp.float32)
    sent = total.astype(jnp.bfloat16)
    here = total[:2]
    for k in (1, 2, 3):
        here = here + lax.ppermute(sent[2 * k : 2 * k + 2], "src", x_step(k)).astype(jnp.float32)
    far = lax.ppermute(here[1].astype(jnp.bfloat16), "src", HALVES)
    return jnp.stack([here[0], far.astype(jnp.float32)])


def per_device(
    source_table,
    source_state,
    target_table,
    target_state,
    relations,
    edge_source,
    edge_target,
    batch_relation,
    edge_counts,
    negatives,
):
    member = lax.axis_index("src").reshape(1)
    source_blocks, target_lines = pack_tables(source_table, target_table)
    sources_all = lax.all_to_all(source_blocks, "dst", 0, 0)
    slots = (1, BATCHES * BATCH)
    lists = (
        batch_relation.reshape(BATCHES),
        edge_counts.reshape(1),
        edge_source.reshape(slots),
        edge_target.reshape(slots),
        negatives.reshape(slots),
    )
    targets_own, targets_other, (n, m) = gather_src(target_lines, counts, lists)
    source_grad, own, other = gradients(member, sources_all, targets_own, targets_other, relations, n, m)
    source_parts = lax.all_to_all(source_grad, "dst", 0, 0)
    target_parts = scatter_src(own, other)
    new_source_table, new_source_state = update(source_parts, source_table, source_state)
    new_target_table, new_target_state = update(target_parts, target_table, target_state)
    return (new_source_table, new_source_state, new_target_table, new_target_state)


def solution(mesh):
    return jax.shard_map(
        per_device,
        mesh=mesh,
        in_specs=(
            P(("src", "dst"), None),
            P(("src", "dst")),
            P(("dst", "src"), None),
            P(("dst", "src")),
            P(),
            P("src", "dst", None),
            P("src", "dst", None),
            P("src", "dst", None),
            P("src", "dst"),
            P("src", "dst", None, None),
        ),
        out_specs=(
            P(("src", "dst"), None),
            P(("src", "dst")),
            P(("dst", "src"), None),
            P(("dst", "src")),
        ),
        check_vma=False,
    )
```
